256 devices in a mesh: lat: 32 (over y, x, core), tok: 8 (over z).
Axes of the slice: x: 4, y: 4, z: 8, core: 2. Of those that a mesh axis runs over, the one named last changes fastest.
Arguments:
- acts_early: bfloat16 [512, 3584], P(('lat', 'tok')), may hold values from -6 to 6
- acts_late: bfloat16 [512, 3584], P(('lat', 'tok')), may hold values from -6 to 6
- enc_early: bfloat16 [3584, 131072], P(None, ('lat', 'tok')), may hold values from -0.09375 to 0.09375
- enc_late: bfloat16 [3584, 131072], P(None, ('lat', 'tok')), may hold values from -0.09375 to 0.09375
- bias_early: float32 [131072], P(('lat', 'tok')), may hold values from -3 to 3
- bias_late: float32 [131072], P(('lat', 'tok')), may hold values from -3 to 3
- thresh_early: float32 [131072], P(('lat', 'tok')), may hold values from 0.1 to 2
- thresh_late: float32 [131072], P(('lat', 'tok')), may hold values from 0.1 to 2
- pair_blocks: int32 [4096, 2], P('lat'), may hold values from 0 to 1023, as said below
- live_pairs: int32 [32], P('lat'), may hold values from 32 to 128, as said below
Outputs:
- gram_tiles: float32 [4096, 128, 128], P(('lat', 'tok'))
The draws below stay inside these ranges and needn't reach their ends.
Inputs may be any that keep to these rules, and one draw needn't show every extreme that they name: `pair_blocks`: block numbers count blocks of 128 latents; latent group g holds blocks g * 32 to g * 32 + 31. In each column, the 128 rows of one owner name every latent group exactly 4 times. `live_pairs`: some owner has all 128 slots live.
All inputs are finite; a program needn't handle non-finite values.
Results may differ from the reference program's by a relative error of at most 0.00035.
Values may be sent and summed in bfloat16 or wider, within the bound.
No kernel may reach another device: no remote copies, remote signals or barrier semaphores. Data moves between devices by JAX's collectives and lax.ppermute only.
A program may use at most 64 MiB of HBM per device.

```python
import math
import jax
import jax.numpy as jnp
from jax import lax

D = 3584
LAT = 131072
BLOCK = 128
FROM_GROUP = 4
TOKENS = 512
SLOTS = 128
N_LAT = 32


def block_column(key):
    group_blocks = LAT // (N_LAT * BLOCK)
    order_keys = jax.random.split(key, N_LAT)
    tickets = jax.vmap(lambda sub: jax.random.permutation(sub, SLOTS))(order_keys)
    source = tickets // FROM_GROUP
    within = jax.random.randint(jax.random.fold_in(key, 7), (N_LAT, SLOTS), 0, group_blocks)
    return (source * group_blocks + within).reshape(N_LAT * SLOTS)


def draw_pair_blocks(key, part):
    key = jax.random.fold_in(key, 5)
    first = block_column(jax.random.fold_in(key, 1))
    second = block_column(jax.random.fold_in(key, 2))
    return jnp.stack([first, second], axis=1).astype(jnp.int32)


def draw_live_pairs(key, part):
    key = jax.random.fold_in(key, 9)
    counts = jax.random.randint(jax.random.fold_in(key, 1), (N_LAT,), SLOTS // 4, SLOTS * 5 // 8 + 1)
    fullest = jax.random.randint(jax.random.fold_in(key, 3), (), 0, N_LAT)
    return jnp.where(jnp.arange(N_LAT) == fullest, SLOTS, counts).astype(jnp.int32)


def levels(key, extent, pieces, least, top_value):
    def one(axis_at, blocks):
        steps = jax.random.uniform(jax.random.fold_in(jax.random.fold_in(key, 6), axis_at), (blocks,), jnp.float32, least / len(pieces), top_value / len(pieces))
        return jnp.repeat(jnp.exp(steps), extent[axis_at] // blocks).reshape((-1,) + (1,) * (len(extent) - axis_at - 1))

    gain = one(*pieces[0])
    for cut in pieces[1:]:
        gain = gain * one(*cut)
    return gain


def centred(rng, extent, spread, bound, cuts=(), kind=jnp.bfloat16):
    gain = levels(rng, extent, cuts, -0.22, 0.18) if cuts else 1.0
    values = jax.random.normal(rng, extent, jnp.float32) * spread * gain
    return jnp.minimum(jnp.maximum(values, -bound), bound).astype(kind)


def setup_inputs(seed: int = 0) -> dict:
    seeds = jax.random.split(jax.random.key(seed), 11)
    return {
        "acts_early": centred(seeds[0], (TOKENS, D), 1.0, 6.0, ((0, 256),)),
        "acts_late": centred(seeds[1], (TOKENS, D), 1.0, 6.0, ((0, 256),)),
        "enc_early": centred(seeds[2], (D, LAT), D ** -0.5, 0.09375, ((1, 256),)),
        "enc_late": centred(seeds[3], (D, LAT), D ** -0.5, 0.09375, ((1, 256),)),
        "bias_early": centred(seeds[4], (LAT,), 1.0, 3.0, ((0, 256),), jnp.float32),
        "bias_late": centred(seeds[5], (LAT,), 1.0, 3.0, ((0, 256),), jnp.float32),
        "thresh_early": jnp.clip(jnp.exp(math.log(2.0) - 2.9957323 * jax.random.uniform(seeds[6], (LAT,), jnp.float32) ** levels(seeds[6], (LAT,), ((0, 256),), -0.2, 0.2)), 0.1, 2.0),
        "thresh_late": jnp.clip(jnp.exp(math.log(2.0) - 2.9957323 * jax.random.uniform(seeds[7], (LAT,), jnp.float32) ** levels(seeds[7], (LAT,), ((0, 256),), -0.2, 0.2)), 0.1, 2.0),
        "pair_blocks": draw_pair_blocks(jax.random.fold_in(seeds[10], 71), 0),
        "live_pairs": draw_live_pairs(jax.random.fold_in(seeds[10], 71), 0),
    }


def soft_jump(preact, thresh):
    return preact * jnp.clip(2.0 * preact / thresh - 1.0, 0.0, 1.0)


def encode(acts, weight, bias_vec, thresh):
    preact = jnp.dot(acts, weight, preferred_element_type=jnp.float32) + bias_vec
    return soft_jump(preact, thresh).astype(jnp.bfloat16)


def reference(acts_early, acts_late, enc_early, enc_late, bias_early, bias_late, thresh_early, thresh_late, pair_blocks, live_pairs):
    codes_early = encode(acts_early, enc_early, bias_early, thresh_early).reshape(TOKENS, LAT // BLOCK, BLOCK)
    codes_late = encode(acts_late, enc_late, bias_late, thresh_late).reshape(TOKENS, LAT // BLOCK, BLOCK)
    slot_index = jnp.arange(N_LAT * SLOTS, dtype=jnp.int32)
    is_live = (slot_index % SLOTS) < jnp.repeat(live_pairs, SLOTS)

    def one_tile(entry):
        pair_row, live_flag = entry
        left_block = lax.dynamic_index_in_dim(codes_early, pair_row[0], 1, keepdims=False)
        right_block = lax.dynamic_index_in_dim(codes_late, pair_row[1], 1, keepdims=False)
        gram = jnp.dot(left_block.T, right_block, preferred_element_type=jnp.float32) / TOKENS
        return jnp.where(live_flag, gram, jnp.zeros_like(gram))

    return lax.map(one_tile, (pair_blocks, is_live))
```

```python
import jax
import jax.numpy as jnp
from jax import lax
from jax.experimental import pallas as pl
from jax.experimental.pallas import tpu as pltpu
from jax.sharding import Mesh, PartitionSpec as P

BLOCK = 128
FROM_GROUP = 4
GROUPS = 32
RANKS = 8
TOKENS = 512
ALL = ("y", "x", "c", "z")
LAT = ("y", "x", "c")
MIB = 1 << 20


def encode_kernel(core_ref, own_ref, other_ref, w_ref, bias_ref, thresh_ref, out_ref):
    core = core_ref[0]
    rows = own_ref.shape[0] // RANKS
    for side, acts_ref in enumerate((own_ref, other_ref)):
        half = core if side == 0 else 1 - core
        at = pl.multiple_of(half * rows, rows)
        preact = jnp.dot(acts_ref[...], w_ref[...], preferred_element_type=jnp.float32) + bias_ref[...]
        codes = preact * jnp.clip(2.0 * preact / thresh_ref[...] - 1.0, 0.0, 1.0)
        codes = codes.astype(jnp.bfloat16)
        for t in range(RANKS):
            for j in range(out_ref.shape[1]):
                out_ref[t, j, pl.ds(at, rows), :] = codes[
                    t * rows : (t + 1) * rows, j * BLOCK : (j + 1) * BLOCK
                ]


def encode(core, own, other, weight, bias_vec, thresh):
    half, depth = own.shape
    width = weight.shape[1]
    step = 256
    return pl.pallas_call(
        encode_kernel,
        grid_spec=pltpu.PrefetchScalarGridSpec(
            num_scalar_prefetch=1,
            grid=(width // step,),
            in_specs=[
                pl.BlockSpec((half, depth), lambda i, s: (0, 0)),
                pl.BlockSpec((half, depth), lambda i, s: (0, 0)),
                pl.BlockSpec((depth, step), lambda i, s: (0, i)),
                pl.BlockSpec((1, step), lambda i, s: (0, i)),
                pl.BlockSpec((1, step), lambda i, s: (0, i)),
            ],
            out_specs=pl.BlockSpec(
                (RANKS, step // BLOCK, 2 * half // RANKS, BLOCK), lambda i, s: (0, i, 0, 0)
            ),
        ),
        out_shape=jax.ShapeDtypeStruct(
            (RANKS, width // BLOCK, 2 * half // RANKS, BLOCK), jnp.bfloat16
        ),
        compiler_params=pltpu.CompilerParams(vmem_limit_bytes=24 * MIB),
        cost_estimate=pl.CostEstimate(
            flops=4 * half * depth * width, bytes_accessed=8 * MIB, transcendentals=0
        ),
        name="encode",
    )(core, own, other, weight, bias_vec[None], thresh[None])


def pick_kernel(index_ref, blocks_ref, out_ref):
    def body(i, carry):
        out_ref[i] = blocks_ref[index_ref[i]]
        return carry

    lax.fori_loop(0, out_ref.shape[0], body, 0, unroll=8)


def pick(index, blocks):
    count = index.shape[0]
    return pl.pallas_call(
        pick_kernel,
        in_specs=[
            pl.BlockSpec(memory_space=pltpu.SMEM),
            pl.BlockSpec(memory_space=pltpu.VMEM),
        ],
        out_specs=pl.BlockSpec(memory_space=pltpu.VMEM),
        out_shape=jax.ShapeDtypeStruct((count,) + blocks.shape[1:], blocks.dtype),
        compiler_params=pltpu.CompilerParams(vmem_limit_bytes=16 * MIB),
        cost_estimate=pl.CostEstimate(flops=0, bytes_accessed=3 * MIB, transcendentals=0),
        name="pick",
    )(index, blocks)


def tile_kernel(left_at, right_at, live_ref, left_ref, right_ref, out_ref):
    count = out_ref.shape[0]
    first = pl.program_id(0) * count
    live = live_ref[0]
    for i in range(count):
        slot = first + i

        @pl.when(slot < live)
        def _():
            gram = lax.dot_general(
                left_ref[left_at[slot]],
                right_ref[right_at[slot]],
                (((0,), (0,)), ((), ())),
                preferred_element_type=jnp.float32,
            )
            out_ref[i] = gram * (1.0 / TOKENS)

        @pl.when(slot >= live)
        def _():
            out_ref[i] = jnp.zeros(out_ref.shape[1:], jnp.float32)


def tiles(left_at, right_at, live, left, right):
    slots = left_at.shape[0]
    step = slots // RANKS
    return pl.pallas_call(
        tile_kernel,
        grid_spec=pltpu.PrefetchScalarGridSpec(
            num_scalar_prefetch=3,
            grid=(slots // step,),
            in_specs=[
                pl.BlockSpec(left.shape, lambda i, *s: (0, 0, 0)),
                pl.BlockSpec(right.shape, lambda i, *s: (0, 0, 0)),
            ],
            out_specs=pl.BlockSpec((step, BLOCK, BLOCK), lambda i, *s: (i, 0, 0)),
        ),
        out_shape=jax.ShapeDtypeStruct((slots, BLOCK, BLOCK), jnp.float32),
        compiler_params=pltpu.CompilerParams(vmem_limit_bytes=24 * MIB),
        cost_estimate=pl.CostEstimate(
            flops=2 * slots * 64 * BLOCK * BLOCK, bytes_accessed=12 * MIB, transcendentals=0
        ),
        name="tiles",
    )(left_at, right_at, live, left, right)


def positions(pair_blocks, group_blocks):
    source = pair_blocks // group_blocks
    within = pair_blocks % group_blocks
    slots = pair_blocks.shape[0]
    order = jnp.arange(slots)
    same = source[:, None, :] == source[None, :, :]
    before = (order[None, :] < order[:, None])[:, :, None]
    rank = jnp.sum(same & before, axis=1, dtype=jnp.int32)
    position = source * FROM_GROUP + rank
    hit = position[None, :, :] == order[:, None, None]
    table = jnp.sum(jnp.where(hit, within[None, :, :], 0), axis=1, dtype=jnp.int32)
    return position, table


def gather_z(acts):
    spread = jnp.broadcast_to(acts[None], (RANKS,) + acts.shape)
    return lax.all_to_all(spread, "z", 0, 0, tiled=True)


def shards(
    acts_early,
    acts_late,
    enc_early,
    enc_late,
    bias_early,
    bias_late,
    thresh_early,
    thresh_late,
    pair_blocks,
    live_pairs,
):
    core = lax.axis_index("c").astype(jnp.int32)[None]
    swap = [(0, 1), (1, 0)]
    depth = acts_early.shape[1]
    group_blocks = RANKS * enc_early.shape[1] // BLOCK

    near = gather_z(jnp.stack([acts_early, acts_late]))
    position, table = positions(pair_blocks, group_blocks)
    asked = lax.all_to_all(
        table.reshape(GROUPS, FROM_GROUP * 2), LAT, split_axis=0, concat_axis=0, tiled=True
    ).reshape(GROUPS * FROM_GROUP, 2)

    picked = []
    for layer, (weight, bias_vec, thresh) in enumerate(
        ((enc_early, bias_early, thresh_early), (enc_late, bias_late, thresh_late))
    ):
        own = lax.all_gather(
            near[:, layer].reshape(-1, depth), ("y", "x"), axis=0, tiled=True
        )
        other = lax.ppermute(own, "c", swap)
        codes = encode(core, own, other, weight, bias_vec, thresh)
        codes = lax.all_to_all(codes, "z", split_axis=0, concat_axis=0, tiled=True)
        blocks = codes.reshape((group_blocks,) + codes.shape[2:])
        sent = pick(asked[:, layer], blocks)
        got = lax.all_to_all(
            sent.reshape((GROUPS, FROM_GROUP) + sent.shape[1:]),
            LAT,
            split_axis=0,
            concat_axis=0,
            tiled=True,
        )
        picked.append(got.reshape(sent.shape))

    sums = tiles(position[:, 0], position[:, 1], live_pairs, picked[0], picked[1])
    return lax.psum_scatter(sums, "z", scatter_dimension=0, tiled=True)


def solution(mesh):
    fine = Mesh(mesh.devices.reshape(4, 4, 2, RANKS), ALL)
    in_specs = (
        P(ALL, None),
        P(ALL, None),
        P(None, ALL),
        P(None, ALL),
        P(ALL),
        P(ALL),
        P(ALL),
        P(ALL),
        P(LAT, None),
        P(LAT),
    )
    out_specs = P(ALL, None, None)
    return jax.shard_map(shards, mesh=fine, in_specs=in_specs, out_specs=out_specs, check_vma=False)
```

```python
import functools

import jax
import jax.numpy as jnp
from jax import lax
from jax.experimental import pallas as pl
from jax.experimental.pallas import tpu as pltpu
from jax.sharding import Mesh, PartitionSpec as P

BLOCK = 128
FROM_GROUP = 4
GROUPS = 32
RANKS = 8
TOKENS = 512
SIDE = 4
CHIPS = SIDE * SIDE
HALF = 8
REACH = 3
ALL = ("y", "x", "c", "z")
LAT = ("y", "x", "c")
MIB = 1 << 20


def activate(preact, bias, thresh):
    preact = preact + bias
    return (preact * jnp.clip(2.0 * preact / thresh - 1.0, 0.0, 1.0)).astype(jnp.bfloat16)


def encode_kernel(place_ref, own_ref, other_ref, w_ref, bias_ref, thresh_ref, out_ref):
    piece = own_ref.shape[0] // CHIPS
    for side, acts_ref in enumerate((own_ref, other_ref)):
        preact = jnp.dot(acts_ref[...], w_ref[...], preferred_element_type=jnp.float32)
        codes = activate(preact, bias_ref[...], thresh_ref[...])
        for u in range(CHIPS):
            rank = place_ref[2 * u]
            at = pl.multiple_of(place_ref[2 * u + 1] ^ (side * piece), piece)
            for j in range(out_ref.shape[1]):
                out_ref[rank, j, pl.ds(at, piece), :] = codes[
                    u * piece : (u + 1) * piece, j * BLOCK : (j + 1) * BLOCK
                ]


def encode_pieces(place, own, other, weight, bias_vec, thresh):
    half, depth = own.shape
    width = weight.shape[1]
    step = 256
    return pl.pallas_call(
        encode_kernel,
        grid_spec=pltpu.PrefetchScalarGridSpec(
            num_scalar_prefetch=1,
            grid=(width // step,),
            in_specs=[
                pl.BlockSpec((half, depth), lambda i, s: (0, 0)),
                pl.BlockSpec((half, depth), lambda i, s: (0, 0)),
                pl.BlockSpec((depth, step), lambda i, s: (0, i)),
                pl.BlockSpec((1, step), lambda i, s: (0, i)),
                pl.BlockSpec((1, step), lambda i, s: (0, i)),
            ],
            out_specs=pl.BlockSpec(
                (RANKS, step // BLOCK, 2 * half // RANKS, BLOCK), lambda i, s: (0, i, 0, 0)
            ),
        ),
        out_shape=jax.ShapeDtypeStruct(
            (RANKS, width // BLOCK, 2 * half // RANKS, BLOCK), jnp.bfloat16
        ),
        compiler_params=pltpu.CompilerParams(vmem_limit_bytes=24 * MIB),
        cost_estimate=pl.CostEstimate(
            flops=4 * half * depth * width, bytes_accessed=8 * MIB, transcendentals=0
        ),
        name="encode_pieces",
    )(place, own, other, weight, bias_vec[None], thresh[None])


def encode_rows_kernel(acts_ref, w_ref, bias_ref, thresh_ref, out_ref):
    rows = out_ref.shape[2]
    preact = jnp.dot(acts_ref[...], w_ref[...], preferred_element_type=jnp.float32)
    codes = activate(preact, bias_ref[...], thresh_ref[...])
    for t in range(RANKS):
        for j in range(out_ref.shape[1]):
            out_ref[t, j] = codes[t * rows : (t + 1) * rows, j * BLOCK : (j + 1) * BLOCK]


def encode_rows(acts, weight, bias_vec, thresh):
    tokens, depth = acts.shape
    width = weight.shape[1]
    step = 256
    return pl.pallas_call(
        encode_rows_kernel,
        grid=(width // step,),
        in_specs=[
            pl.BlockSpec((tokens, depth), lambda i: (0, 0)),
            pl.BlockSpec((depth, step), lambda i: (0, i)),
            pl.BlockSpec((1, step), lambda i: (0, i)),
            pl.BlockSpec((1, step), lambda i: (0, i)),
        ],
        out_specs=pl.BlockSpec((RANKS, step // BLOCK, tokens // RANKS, BLOCK), lambda i: (0, i, 0, 0)),
        out_shape=jax.ShapeDtypeStruct((RANKS, width // BLOCK, tokens // RANKS, BLOCK), jnp.bfloat16),
        compiler_params=pltpu.CompilerParams(vmem_limit_bytes=24 * MIB),
        cost_estimate=pl.CostEstimate(
            flops=2 * tokens * depth * width, bytes_accessed=8 * MIB, transcendentals=0
        ),
        name="encode_rows",
    )(acts, weight, bias_vec[None], thresh[None])


def pick_kernel(index_ref, blocks_ref, out_ref):
    def body(i, carry):
        out_ref[i] = blocks_ref[index_ref[i]]
        return carry

    lax.fori_loop(0, out_ref.shape[0], body, 0, unroll=8)


def pick(index, blocks):
    count = index.shape[0]
    return pl.pallas_call(
        pick_kernel,
        in_specs=[
            pl.BlockSpec(memory_space=pltpu.SMEM),
            pl.BlockSpec(memory_space=pltpu.VMEM),
        ],
        out_specs=pl.BlockSpec(memory_space=pltpu.VMEM),
        out_shape=jax.ShapeDtypeStruct((count,) + blocks.shape[1:], blocks.dtype),
        compiler_params=pltpu.CompilerParams(vmem_limit_bytes=16 * MIB),
        cost_estimate=pl.CostEstimate(flops=0, bytes_accessed=3 * MIB, transcendentals=0),
        name="pick",
    )(index, blocks)


def route_kernel(slot_ref, at_ref, blocks_ref, *outs):
    for side in range(2):
        for k in range(REACH + 1):
            out_ref = outs[side * (REACH + 1) + k]
            for part in range(2):
                first = slot_ref[(side * (REACH + 1) + k) * 2 + part]
                for i in range(HALF):
                    out_ref[part * HALF + i] = blocks_ref[at_ref[first + i]]


def route(slot, at, blocks):
    one = jax.ShapeDtypeStruct((2 * HALF,) + blocks.shape[1:], blocks.dtype)
    count = 2 * (REACH + 1)
    return pl.pallas_call(
        route_kernel,
        in_specs=[
            pl.BlockSpec(memory_space=pltpu.SMEM),
            pl.BlockSpec(memory_space=pltpu.SMEM),
            pl.BlockSpec(memory_space=pltpu.VMEM),
        ],
        out_specs=[pl.BlockSpec(memory_space=pltpu.VMEM)] * count,
        out_shape=[one] * count,
        compiler_params=pltpu.CompilerParams(vmem_limit_bytes=16 * MIB),
        cost_estimate=pl.CostEstimate(flops=0, bytes_accessed=4 * MIB, transcendentals=0),
        name="route",
    )(slot, at, blocks)


def gram_sum(lefts, rights, i):
    total = None
    for left_ref, right_ref in zip(lefts, rights):
        gram = lax.dot_general(
            left_ref[i], right_ref[i], (((0,), (0,)), ((), ())), preferred_element_type=jnp.float32
        )
        total = gram if total is None else total + gram
    return total


def half_tiles_kernel(first, *refs):
    out_refs = refs[-2:]
    refs = refs[:-2]
    count = REACH + 1
    for side in range(2):
        lefts = refs[side * count : (side + 1) * count]
        rights = refs[(2 + side) * count : (3 + side) * count]
        for i in range(HALF):
            out_refs[side][i] = gram_sum(lefts, rights, first + i)


def half_tiles(first, lefts, rights):
    one = jax.ShapeDtypeStruct((HALF, BLOCK, BLOCK), jnp.float32)
    count = 4 * (REACH + 1)
    return pl.pallas_call(
        functools.partial(half_tiles_kernel, first),
        in_specs=[pl.BlockSpec(memory_space=pltpu.VMEM)] * count,
        out_specs=[pl.BlockSpec(memory_space=pltpu.VMEM)] * 2,
        out_shape=[one] * 2,
        compiler_params=pltpu.CompilerParams(vmem_limit_bytes=16 * MIB),
        cost_estimate=pl.CostEstimate(
            flops=2 * 16 * 256 * BLOCK * BLOCK, bytes_accessed=3 * MIB, transcendentals=0
        ),
        name="half_tiles",
    )(*lefts, *rights)


def finish_kernel(first_ref, live_ref, low_ref, low_far_ref, high_ref, high_far_ref, out_ref):
    for i in range(2 * HALF):
        near_ref, far_ref = (low_ref, low_far_ref) if i < HALF else (high_ref, high_far_ref)
        total = (near_ref[i % HALF] + far_ref[i % HALF]) * (1.0 / TOKENS)
        out_ref[i] = jnp.where(first_ref[0] + i < live_ref[0], total, 0.0)


def finish(first, live, low, low_far, high, high_far):
    return pl.pallas_call(
        finish_kernel,
        in_specs=[pl.BlockSpec(memory_space=pltpu.SMEM)] * 2
        + [pl.BlockSpec(memory_space=pltpu.VMEM)] * 4,
        out_specs=pl.BlockSpec(memory_space=pltpu.VMEM),
        out_shape=jax.ShapeDtypeStruct((2 * HALF, BLOCK, BLOCK), jnp.float32),
        compiler_params=pltpu.CompilerParams(vmem_limit_bytes=16 * MIB),
        cost_estimate=pl.CostEstimate(flops=MIB, bytes_accessed=3 * MIB, transcendentals=0),
        name="finish",
    )(first, live, low, low_far, high, high_far)


def positions(pair_blocks, group_blocks):
    source = pair_blocks // group_blocks
    within = pair_blocks % group_blocks
    slots = pair_blocks.shape[0]
    order = jnp.arange(slots)
    same = source[:, None, :] == source[None, :, :]
    before = (order[None, :] < order[:, None])[:, :, None]
    rank = jnp.sum(same & before, axis=1, dtype=jnp.int32)
    position = source * FROM_GROUP + rank
    hit = position[None, :, :] == order[:, None, None]
    table = jnp.sum(jnp.where(hit, within[None, :, :], 0), axis=1, dtype=jnp.int32)
    return position, table


def shift(value, axis, size, by):
    return lax.ppermute(value, axis, [(i, (i + by) % size) for i in range(size)])


def gather_z(acts):
    spread = jnp.broadcast_to(acts[None], (RANKS,) + acts.shape)
    return lax.all_to_all(spread, "z", 0, 0, tiled=True)


def ring_of_four(value, axis):
    return [value] + [shift(value, axis, SIDE, k) for k in range(1, SIDE)]


def gather_chips(rows):
    width = rows.shape[1] // 2
    left, right = rows[:, :width], rows[:, width:]
    left_x = jnp.stack(ring_of_four(left, "x"))
    right_y = jnp.stack(ring_of_four(right, "y"))
    left_all = jnp.stack(ring_of_four(left_x, "y"))
    right_all = jnp.stack(ring_of_four(right_y, "x"), axis=1)
    return jnp.concatenate([left_all, right_all], axis=3).reshape(-1, rows.shape[1])


def shards(
    acts_early,
    acts_late,
    enc_early,
    enc_late,
    bias_early,
    bias_late,
    thresh_early,
    thresh_late,
    pair_blocks,
    live_pairs,
):
    y, x, c, z = (lax.axis_index(name).astype(jnp.int32) for name in ALL)
    depth = acts_early.shape[1]
    group_blocks = RANKS * enc_early.shape[1] // BLOCK

    near = gather_z(jnp.stack([acts_early, acts_late]))
    rows_early = near[:, 0].reshape(-1, depth)
    rows_late = near[:, 1].reshape(-1, depth)
    all_late = lax.all_gather(rows_late, LAT, axis=0, tiled=True)

    position, table = positions(pair_blocks, group_blocks)
    asked = lax.all_to_all(
        table.reshape(GROUPS, FROM_GROUP * 2), LAT, split_axis=0, concat_axis=0, tiled=True
    ).reshape(GROUPS * FROM_GROUP, 2)

    own = gather_chips(rows_early)
    other = shift(own, "c", 2, 1)
    step = jnp.arange(SIDE, dtype=jnp.int32)
    chip = ((y - step) % SIDE)[:, None] * SIDE + ((x - step) % SIDE)[None, :]
    chip = chip.reshape(-1)
    place = jnp.stack([chip // 2, (chip % 2) * 32 + c * 16], axis=1).reshape(-1)

    def spread(codes, layer):
        codes = lax.all_to_all(codes, "z", split_axis=0, concat_axis=0, tiled=True)
        sent = pick(asked[:, layer], codes.reshape((group_blocks,) + codes.shape[2:]))
        got = lax.all_to_all(
            sent.reshape((GROUPS, FROM_GROUP) + sent.shape[1:]),
            LAT,
            split_axis=0,
            concat_axis=0,
            tiled=True,
        )
        return got.reshape(sent.shape)

    slots = []
    for side in range(2):
        for k in range(REACH + 1):
            by = k if side == 0 else -k
            past = by + (1 if side == 0 else -1)
            for part, (plane, half) in enumerate(((past, side), (by, 1 - side))):
                slots.append(((z + plane) % RANKS) * (2 * HALF) + half * HALF)
    slots = jnp.stack(slots)

    def trade(blocks, layer):
        parts = route(slots, position[:, layer], blocks)
        out = list(parts)
        for k in range(REACH, 0, -1):
            for side in range(2):
                at = side * (REACH + 1) + k
                out[at] = shift(parts[at], "z", RANKS, k if side == 0 else -k)
        return out

    codes_early = encode_pieces(place, own, other, enc_early, bias_early, thresh_early)
    lefts = trade(spread(codes_early, 0), 0)
    codes_late = encode_rows(all_late, enc_late, bias_late, thresh_late)
    rights = trade(spread(codes_late, 1), 1)

    up, down = half_tiles(0, lefts, rights)
    low_far = shift(up, "z", RANKS, 1)
    high_far = shift(down, "z", RANKS, -1)
    high, low = half_tiles(HALF, lefts, rights)
    return finish((z * (2 * HALF))[None], live_pairs, low, low_far, high, high_far)


def solution(mesh):
    fine = Mesh(mesh.devices.reshape(SIDE, SIDE, 2, RANKS), ALL)
    in_specs = (
        P(ALL, None),
        P(ALL, None),
        P(None, ALL),
        P(None, ALL),
        P(ALL),
        P(ALL),
        P(ALL),
        P(ALL),
        P(LAT, None),
        P(LAT),
    )
    out_specs = P(ALL, None, None)
    return jax.shard_map(shards, mesh=fine, in_specs=in_specs, out_specs=out_specs, check_vma=False)
```

```python
import functools

import jax
import jax.numpy as jnp
from jax import lax
from jax.experimental import pallas as pl
from jax.experimental.pallas import tpu as pltpu
from jax.sharding import Mesh, PartitionSpec as P

BLOCK = 128
FROM_GROUP = 4
GROUPS = 32
RANKS = 8
TOKENS = 512
SIDE = 4
CHIPS = SIDE * SIDE
HALF = 8
REACH = 3
STEP = 256
PICKS = 4
NEXT = (1, 2 + REACH)
ORDER = (3, 7, 2, 6, 1, 5, 0, 4)
ALL = ("y", "x", "c", "z")
LAT = ("y", "x", "c")
MIB = 1 << 20


def activate(preact, bias, thresh):
    preact = preact + bias
    return (preact * jnp.clip(2.0 * preact / thresh - 1.0, 0.0, 1.0)).astype(jnp.bfloat16)


def early_kernel(place_ref, own_ref, other_ref, w_ref, bias_ref, thresh_ref, out_ref):
    piece = own_ref.shape[0] // CHIPS
    for side, acts_ref in enumerate((own_ref, other_ref)):
        preact = jnp.dot(acts_ref[...], w_ref[...], preferred_element_type=jnp.float32)
        codes = activate(preact, bias_ref[...], thresh_ref[...])
        for u in range(CHIPS):
            rank = place_ref[2 * u]
            at = pl.multiple_of(place_ref[2 * u + 1] ^ (side * piece), piece)
            for j in range(out_ref.shape[1]):
                out_ref[rank, j, pl.ds(at, piece), :] = codes[
                    u * piece : (u + 1) * piece, j * BLOCK : (j + 1) * BLOCK
                ]


def late_kernel(plane_ref, acts_ref, w_ref, bias_ref, thresh_ref, *refs):
    codes_ref = refs[-1]
    piece = acts_ref.shape[0] // RANKS
    preact = jnp.dot(acts_ref[...], w_ref[...], preferred_element_type=jnp.float32)
    codes_ref[...] = activate(preact, bias_ref[...], thresh_ref[...])
    for k in range(RANKS):
        at = pl.multiple_of(((plane_ref[0] + k) % RANKS) * piece, piece)
        codes = codes_ref[pl.ds(at, piece), :]
        for j in range(refs[k].shape[0]):
            refs[k][j] = codes[:, j * BLOCK : (j + 1) * BLOCK]


def encode(kernel, name, scalar, acts, weight, bias_vec, thresh, out_shape, scratch=()):
    depth, width = weight.shape
    outs = jax.tree.leaves(out_shape)
    specs = [
        pl.BlockSpec((STEP // BLOCK,) + out.shape[1:], lambda i, s: (i, 0, 0))
        if out.ndim == 3
        else pl.BlockSpec(out.shape[:1] + (STEP // BLOCK,) + out.shape[2:], lambda i, s: (0, i, 0, 0))
        for out in outs
    ]
    return pl.pallas_call(
        kernel,
        grid_spec=pltpu.PrefetchScalarGridSpec(
            num_scalar_prefetch=1,
            grid=(width // STEP,),
            in_specs=[pl.BlockSpec(one.shape, lambda i, s: (0, 0)) for one in acts]
            + [pl.BlockSpec((depth, STEP), lambda i, s: (0, i))]
            + [pl.BlockSpec((1, STEP), lambda i, s: (0, i))] * 2,
            out_specs=specs if isinstance(out_shape, list) else specs[0],
            scratch_shapes=scratch,
        ),
        out_shape=out_shape,
        compiler_params=pltpu.CompilerParams(vmem_limit_bytes=24 * MIB),
        cost_estimate=pl.CostEstimate(
            flops=2 * TOKENS * depth * width, bytes_accessed=8 * MIB, transcendentals=0
        ),
        name=name,
    )(scalar, *acts, weight, bias_vec[None], thresh[None])


def pick_kernel(index_ref, blocks_ref, out_ref, buf_ref, sems):
    chunk = out_ref.shape[0] // PICKS
    copies = []
    for part in range(PICKS):
        for i in range(part * chunk, (part + 1) * chunk):
            buf_ref[i] = blocks_ref[index_ref[i]]
        at = pl.ds(part * chunk, chunk)
        copies.append(pltpu.make_async_copy(buf_ref.at[at], out_ref.at[at], sems.at[part]))
        copies[-1].start()
    for copy in copies:
        copy.wait()


def pick(index, blocks):
    shape = (index.shape[0],) + blocks.shape[1:]
    return pl.pallas_call(
        pick_kernel,
        in_specs=[
            pl.BlockSpec(memory_space=pltpu.SMEM),
            pl.BlockSpec(memory_space=pltpu.VMEM),
        ],
        out_specs=pl.BlockSpec(memory_space=pltpu.HBM),
        out_shape=pltpu.HBM(shape, blocks.dtype),
        scratch_shapes=[pltpu.VMEM(shape, blocks.dtype), pltpu.SemaphoreType.DMA((PICKS,))],
        compiler_params=pltpu.CompilerParams(vmem_limit_bytes=16 * MIB),
        cost_estimate=pl.CostEstimate(flops=0, bytes_accessed=3 * MIB, transcendentals=0),
        name="pick",
    )(index, blocks)


def route_kernel(extras, slot_ref, at_ref, blocks_ref, *refs):
    extra_refs, refs = refs[:extras], refs[extras:]
    outs, (buf_ref, sems) = refs[:-2], refs[-2:]
    copies = []
    for n, out_ref in enumerate(outs):
        extra = 2 * HALF if extras and n in NEXT else 0
        if extra:
            copies.append(
                pltpu.make_async_copy(
                    extra_refs[NEXT.index(n)], out_ref.at[pl.ds(0, extra)], sems.at[len(outs) + NEXT.index(n)]
                )
            )
            copies[-1].start()
    for n in ORDER:
        extra = 2 * HALF if extras and n in NEXT else 0
        for part in range(2):
            first = slot_ref[2 * n + part]
            for i in range(HALF):
                buf_ref[n, part * HALF + i] = blocks_ref[at_ref[first + i]]
        copies.append(
            pltpu.make_async_copy(buf_ref.at[n], outs[n].at[pl.ds(extra, 2 * HALF)], sems.at[n])
        )
        copies[-1].start()
    for copy in copies:
        copy.wait()


def route(slot, at, blocks, extras=()):
    count = 2 * (REACH + 1)
    tail = blocks.shape[1:]
    return pl.pallas_call(
        functools.partial(route_kernel, len(extras)),
        in_specs=[
            pl.BlockSpec(memory_space=pltpu.SMEM),
            pl.BlockSpec(memory_space=pltpu.SMEM),
            pl.BlockSpec(memory_space=pltpu.VMEM),
        ]
        + [pl.BlockSpec(memory_space=pl.ANY)] * len(extras),
        out_specs=[pl.BlockSpec(memory_space=pltpu.HBM)] * count,
        out_shape=[
            pltpu.HBM((2 * HALF * (2 if extras and n in NEXT else 1),) + tail, blocks.dtype)
            for n in range(count)
        ],
        scratch_shapes=[
            pltpu.VMEM((count, 2 * HALF) + tail, blocks.dtype),
            pltpu.SemaphoreType.DMA((count + 2,)),
        ],
        compiler_params=pltpu.CompilerParams(vmem_limit_bytes=16 * MIB),
        cost_estimate=pl.CostEstimate(flops=0, bytes_accessed=4 * MIB, transcendentals=0),
        name="route",
    )(slot, at, blocks, *extras)


def gram_kernel(lows, *refs):
    out_ref = refs[-1]
    count = REACH + 1
    for i in range(HALF):
        left, right = (
            jnp.concatenate([refs[n][lows[n] + i] for n in range(base, base + count)], axis=0)
            for base in (0, count)
        )
        out_ref[i] = lax.dot_general(
            left, right, (((0,), (0,)), ((), ())), preferred_element_type=jnp.float32
        )


def gram(lows, parts):
    return pl.pallas_call(
        functools.partial(gram_kernel, lows),
        in_specs=[pl.BlockSpec(memory_space=pltpu.VMEM)] * len(parts),
        out_specs=pl.BlockSpec(memory_space=pltpu.VMEM),
        out_shape=jax.ShapeDtypeStruct((HALF, BLOCK, BLOCK), jnp.float32),
        compiler_params=pltpu.CompilerParams(vmem_limit_bytes=16 * MIB),
        cost_estimate=pl.CostEstimate(
            flops=2 * HALF * 256 * BLOCK * BLOCK, bytes_accessed=2 * MIB, transcendentals=0
        ),
        name="gram",
    )(*parts)


def finish_kernel(first_ref, live_ref, low_ref, low_far_ref, high_ref, high_far_ref, out_ref):
    for i in range(2 * HALF):
        near_ref, far_ref = (low_ref, low_far_ref) if i < HALF else (high_ref, high_far_ref)
        total = (near_ref[i % HALF] + far_ref[i % HALF]) * (1.0 / TOKENS)
        out_ref[i] = jnp.where(first_ref[0] + i < live_ref[0], total, 0.0)


def finish(first, live, low, low_far, high, high_far):
    return pl.pallas_call(
        finish_kernel,
        in_specs=[pl.BlockSpec(memory_space=pltpu.SMEM)] * 2
        + [pl.BlockSpec(memory_space=pltpu.VMEM)] * 4,
        out_specs=pl.BlockSpec(memory_space=pltpu.VMEM),
        out_shape=jax.ShapeDtypeStruct((2 * HALF, BLOCK, BLOCK), jnp.float32),
        compiler_params=pltpu.CompilerParams(vmem_limit_bytes=16 * MIB),
        cost_estimate=pl.CostEstimate(flops=MIB, bytes_accessed=3 * MIB, transcendentals=0),
        name="finish",
    )(first, live, low, low_far, high, high_far)


def positions(pair_blocks, group_blocks):
    source = pair_blocks // group_blocks
    within = pair_blocks % group_blocks
    slots = pair_blocks.shape[0]
    order = jnp.arange(slots)
    same = source[:, None, :] == source[None, :, :]
    before = (order[None, :] < order[:, None])[:, :, None]
    rank = jnp.sum(same & before, axis=1, dtype=jnp.int32)
    position = source * FROM_GROUP + rank
    hit = position[None, :, :] == order[:, None, None]
    table = jnp.sum(jnp.where(hit, within[None, :, :], 0), axis=1, dtype=jnp.int32)
    return position, table


def shift(value, axis, size, by):
    return lax.ppermute(value, axis, [(i, (i + by) % size) for i in range(size)])


def gather_z(acts):
    spread = jnp.broadcast_to(acts[None], (RANKS,) + acts.shape)
    return lax.all_to_all(spread, "z", 0, 0, tiled=True)


def ring_of_four(value, axis):
    return [value] + [shift(value, axis, SIDE, k) for k in range(1, SIDE)]


def gather_chips(rows):
    width = rows.shape[1] // 2
    left, right = rows[:, :width], rows[:, width:]
    left_x = jnp.stack(ring_of_four(left, "x"))
    right_y = jnp.stack(ring_of_four(right, "y"))
    left_all = jnp.stack(ring_of_four(left_x, "y"))
    right_all = jnp.stack(ring_of_four(right_y, "x"), axis=1)
    return jnp.concatenate([left_all, right_all], axis=3).reshape(-1, rows.shape[1])


def shards(
    acts_early,
    acts_late,
    enc_early,
    enc_late,
    bias_early,
    bias_late,
    thresh_early,
    thresh_late,
    pair_blocks,
    live_pairs,
):
    y, x, c, z = (lax.axis_index(name).astype(jnp.int32) for name in ALL)
    depth = acts_early.shape[1]
    width = enc_early.shape[1]
    rank_blocks = width // BLOCK
    group_blocks = RANKS * rank_blocks

    near = gather_z(jnp.stack([acts_early, acts_late]))
    rows_early = near[:, 0].reshape(-1, depth)
    rows_late = near[:, 1].reshape(-1, depth)
    all_late = lax.all_gather(rows_late, LAT, axis=0, tiled=True)

    position, table = positions(pair_blocks, group_blocks)
    asked = lax.all_to_all(
        table.reshape(GROUPS, FROM_GROUP * 2), LAT, split_axis=0, concat_axis=0, tiled=True
    ).reshape(GROUPS * FROM_GROUP, 2)
    asked_late = ((z - asked[:, 1] // rank_blocks) & (RANKS - 1)) * rank_blocks + (
        asked[:, 1] % rank_blocks
    )

    own = gather_chips(rows_early)
    step = jnp.arange(CHIPS, dtype=jnp.int32)
    chip = ((y - step // SIDE) & (SIDE - 1)) * SIDE + ((x - step) & (SIDE - 1))
    place = jnp.stack([chip // 2, (chip & 1) * 32 + c * 16], axis=1).reshape(-1)

    def spread(sent):
        got = lax.all_to_all(
            sent.reshape((GROUPS, FROM_GROUP) + sent.shape[1:]),
            LAT,
            split_axis=0,
            concat_axis=0,
            tiled=True,
        )
        return got.reshape(sent.shape)

    offsets = []
    for side in range(2):
        for k in range(REACH + 1):
            by = k if side == 0 else -k
            past = by + (1 if side == 0 else -1)
            offsets += [(past, side), (by, 1 - side)]
    plane = jnp.array([by for by, half in offsets], jnp.int32)
    half = jnp.array([half for by, half in offsets], jnp.int32)
    slots = ((z + plane) & (RANKS - 1)) * (2 * HALF) + half * HALF

    def trade(parts, k):
        return [shift(part, "z", RANKS, by) for part, by in zip(parts, (k, -k))]

    shape = (rank_blocks, TOKENS // RANKS, BLOCK)
    other = shift(own, "c", 2, 1)
    codes_early = encode(
        early_kernel, "encode_early", place, (own, other), enc_early, bias_early, thresh_early,
        jax.ShapeDtypeStruct((RANKS,) + shape, jnp.bfloat16),
    )
    codes_early = lax.all_to_all(codes_early, "z", split_axis=0, concat_axis=0, tiled=True)
    codes_late = encode(
        late_kernel, "encode_late", z[None], (all_late,), enc_late, bias_late, thresh_late,
        [jax.ShapeDtypeStruct(shape, jnp.bfloat16)] * RANKS,
        [pltpu.VMEM((TOKENS, STEP), jnp.bfloat16)],
    )
    codes_early, codes_late = lax.optimization_barrier((codes_early, codes_late))
    sent_early = pick(asked[:, 0], codes_early.reshape((group_blocks,) + shape[1:]))
    got_early = spread(sent_early)
    codes_late = [codes_late[0]] + [shift(codes_late[k], "z", RANKS, k) for k in range(1, RANKS)]
    sent_late = pick(asked_late, jnp.concatenate(codes_late))
    got_early, sent_late = lax.optimization_barrier((got_early, sent_late))

    def both(parts, k):
        return parts[k], parts[k + REACH + 1]

    parts = route(slots, position[:, 0], got_early)
    sent_late, parts = lax.optimization_barrier((sent_late, parts))
    left = {k: trade(both(parts, k), k) for k in (3, 2)}
    left, got_late = lax.optimization_barrier((left, spread(sent_late)))
    left[0] = both(parts, 0)

    parts = route(slots, position[:, 1], got_late, both(parts, 1))
    right = {k: trade(both(parts, k), k) for k in (3, 2, 1)}
    right[0] = both(parts, 0)
    left[1] = right[1]

    def tiles(side, near):
        low = HALF if near else 0
        parts = [left[k][side] for k in range(REACH + 1)] + [right[k][side] for k in range(REACH + 1)]
        lows = [low] * len(parts)
        lows[REACH + 2] += 2 * HALF
        return gram(tuple(lows), parts)

    low_far = shift(tiles(0, False), "z", RANKS, 1)
    high_far = shift(tiles(1, False), "z", RANKS, -1)
    high = tiles(0, True)
    low = tiles(1, True)
    return finish((z * (2 * HALF))[None], live_pairs, low, low_far, high, high_far)


def solution(mesh):
    fine = Mesh(mesh.devices.reshape(SIDE, SIDE, 2, RANKS), ALL)
    in_specs = (
        P(ALL, None),
        P(ALL, None),
        P(None, ALL),
        P(None, ALL),
        P(ALL),
        P(ALL),
        P(ALL),
        P(ALL),
        P(LAT, None),
        P(LAT),
    )
    out_specs = P(ALL, None, None)
    return jax.shard_map(shards, mesh=fine, in_specs=in_specs, out_specs=out_specs, check_vma=False)
```

```python
import functools

import jax
import jax.numpy as jnp
from jax import lax
from jax.experimental import pallas as pl
from jax.experimental.pallas import tpu as pltpu
from jax.sharding import Mesh, PartitionSpec as P

BLOCK = 128
FROM_GROUP = 4
GROUPS = 32
RANKS = 8
TOKENS = 512
SIDE = 4
CHIPS = SIDE * SIDE
HALF = 8
REACH = 3
STEP = 256
PICKS = 4
EARLY_PIECES = 1
LATE_PIECES = 1
NEXT = (1, 2 + REACH)
ORDER = (3, 7, 2, 6, 1, 5, 0, 4)
ALL = ("y", "x", "c", "z")
LAT = ("y", "x", "c")
MIB = 1 << 20


def in_hbm(array):
    return pltpu.with_memory_space_constraint(array, pltpu.HBM)


def activate(preact, bias, thresh):
    preact = preact + bias
    return (preact * jnp.clip(2.0 * preact / thresh - 1.0, 0.0, 1.0)).astype(jnp.bfloat16)


def early_kernel(place_ref, own_ref, other_ref, w_ref, bias_ref, thresh_ref, out_ref):
    piece = own_ref.shape[0] // CHIPS
    for side, acts_ref in enumerate((own_ref, other_ref)):
        preact = jnp.dot(acts_ref[...], w_ref[...], preferred_element_type=jnp.float32)
        codes = activate(preact, bias_ref[...], thresh_ref[...])
        for u in range(CHIPS):
            rank = place_ref[2 * u]
            at = pl.multiple_of(place_ref[2 * u + 1] ^ (side * piece), piece)
            for j in range(out_ref.shape[1]):
                out_ref[rank, j, pl.ds(at, piece), :] = codes[
                    u * piece : (u + 1) * piece, j * BLOCK : (j + 1) * BLOCK
                ]


def late_kernel(plane_ref, acts_ref, w_ref, bias_ref, thresh_ref, *refs):
    codes_ref = refs[-1]
    piece = acts_ref.shape[0] // RANKS
    preact = jnp.dot(acts_ref[...], w_ref[...], preferred_element_type=jnp.float32)
    codes_ref[...] = activate(preact, bias_ref[...], thresh_ref[...])
    for k in range(RANKS):
        at = pl.multiple_of(((plane_ref[0] + k) % RANKS) * piece, piece)
        codes = codes_ref[pl.ds(at, piece), :]
        for j in range(refs[k].shape[0]):
            refs[k][j] = codes[:, j * BLOCK : (j + 1) * BLOCK]


def encode(kernel, name, scalar, acts, weight, bias_vec, thresh, out_shape, scratch=()):
    depth, width = weight.shape
    outs = jax.tree.leaves(out_shape)
    specs = [
        pl.BlockSpec((STEP // BLOCK,) + out.shape[1:], lambda i, s: (i, 0, 0))
        if out.ndim == 3
        else pl.BlockSpec(out.shape[:1] + (STEP // BLOCK,) + out.shape[2:], lambda i, s: (0, i, 0, 0))
        for out in outs
    ]
    return pl.pallas_call(
        kernel,
        grid_spec=pltpu.PrefetchScalarGridSpec(
            num_scalar_prefetch=1,
            grid=(width // STEP,),
            in_specs=[pl.BlockSpec((one.shape[0], depth), lambda i, s: (0, 0)) for one in acts]
            + [pl.BlockSpec((depth, STEP), lambda i, s: (0, i))]
            + [pl.BlockSpec((1, STEP), lambda i, s: (0, i))] * 2,
            out_specs=specs if isinstance(out_shape, list) else specs[0],
            scratch_shapes=scratch,
        ),
        out_shape=out_shape,
        compiler_params=pltpu.CompilerParams(vmem_limit_bytes=24 * MIB),
        cost_estimate=pl.CostEstimate(
            flops=2 * TOKENS * depth * width, bytes_accessed=8 * MIB, transcendentals=0
        ),
        name=name,
    )(scalar, *acts, in_hbm(weight), bias_vec[None], thresh[None])


def pick_kernel(index_ref, blocks_ref, *refs):
    outs, (buf_ref, sems) = refs[:-2], refs[-2:]
    chunk = index_ref.shape[0] // PICKS
    tokens = outs[0].shape[1]
    copies = []
    for n, out_ref in enumerate(outs):
        for part in range(PICKS):
            for i in range(part * chunk, (part + 1) * chunk):
                buf_ref[n, i] = blocks_ref[index_ref[i], n * tokens : (n + 1) * tokens, :]
            at = pl.ds(part * chunk, chunk)
            copies.append(
                pltpu.make_async_copy(buf_ref.at[n, at], out_ref.at[at], sems.at[n * PICKS + part])
            )
            copies[-1].start()
    for copy in copies:
        copy.wait()


def pick(index, blocks, pieces):
    count, (tokens, width) = index.shape[0], blocks.shape[1:]
    shape = (count, tokens // pieces, width)
    return pl.pallas_call(
        pick_kernel,
        in_specs=[
            pl.BlockSpec(memory_space=pltpu.SMEM),
            pl.BlockSpec(memory_space=pltpu.VMEM),
        ],
        out_specs=[pl.BlockSpec(memory_space=pltpu.HBM)] * pieces,
        out_shape=[pltpu.HBM(shape, blocks.dtype)] * pieces,
        scratch_shapes=[
            pltpu.VMEM((pieces,) + shape, blocks.dtype),
            pltpu.SemaphoreType.DMA((pieces * PICKS,)),
        ],
        compiler_params=pltpu.CompilerParams(vmem_limit_bytes=16 * MIB),
        cost_estimate=pl.CostEstimate(flops=0, bytes_accessed=3 * MIB, transcendentals=0),
        name="pick",
    )(index, blocks)


def route_kernel(extras, slot_ref, at_ref, blocks_ref, *refs):
    extra_refs, refs = refs[:extras], refs[extras:]
    count = 2 * (REACH + 1)
    outs, buf_ref, holds, sems = refs[:count], refs[count], refs[count + 1 : -1], refs[-1]
    arriving = [
        pltpu.make_async_copy(extra_ref, holds[m], sems.at[count + m])
        for m, extra_ref in enumerate(extra_refs)
    ]
    for copy in arriving:
        copy.start()
    copies = []
    for n in ORDER:
        for part in range(2):
            first = slot_ref[2 * n + part]
            for i in range(HALF):
                buf_ref[n, part * HALF + i] = blocks_ref[at_ref[first + i]]
        kept = outs[n].shape[0] - 2 * HALF
        copies.append(
            pltpu.make_async_copy(buf_ref.at[n], outs[n].at[pl.ds(kept, 2 * HALF)], sems.at[n])
        )
        copies[-1].start()
    for m, copy in enumerate(arriving):
        copy.wait()
        rows = pl.ds(0, holds[m].shape[0])
        copies.append(
            pltpu.make_async_copy(holds[m], outs[NEXT[m]].at[rows], sems.at[count + extras + m])
        )
        copies[-1].start()
    for copy in copies:
        copy.wait()


def route(slot, at, blocks, extras=()):
    count = 2 * (REACH + 1)
    tail = blocks.shape[1:]
    rows = [2 * HALF] * count
    for m, extra in enumerate(extras):
        rows[NEXT[m]] += extra.shape[0]
    return pl.pallas_call(
        functools.partial(route_kernel, len(extras)),
        in_specs=[
            pl.BlockSpec(memory_space=pltpu.SMEM),
            pl.BlockSpec(memory_space=pltpu.SMEM),
            pl.BlockSpec(memory_space=pltpu.VMEM),
        ]
        + [pl.BlockSpec(memory_space=pl.ANY)] * len(extras),
        out_specs=[pl.BlockSpec(memory_space=pltpu.HBM)] * count,
        out_shape=[pltpu.HBM((row,) + tail, blocks.dtype) for row in rows],
        scratch_shapes=[
            pltpu.VMEM((count, 2 * HALF) + tail, blocks.dtype),
            *(pltpu.VMEM(extra.shape, extra.dtype) for extra in extras),
            pltpu.SemaphoreType.DMA((count + 2 * len(extras),)),
        ],
        compiler_params=pltpu.CompilerParams(vmem_limit_bytes=16 * MIB),
        cost_estimate=pl.CostEstimate(flops=0, bytes_accessed=4 * MIB, transcendentals=0),
        name="route",
    )(slot, at, blocks, *map(in_hbm, extras))


def gram_kernel(layout, lefts, *refs):
    count = len(layout)
    sources, out_ref, bufs, sems = refs[:count], refs[count], refs[count + 1 : -1], refs[-1]
    copies = []
    for n, (low, stride) in enumerate(layout):
        copies.append(
            pltpu.make_async_copy(sources[n].at[pl.ds(low, HALF * stride)], bufs[n], sems.at[n])
        )
        copies[-1].start()
    for copy in copies:
        copy.wait()
    for i in range(HALF):
        left, right = (
            jnp.concatenate(
                [bufs[n][i * layout[n][1] + j] for n in some for j in range(layout[n][1])], axis=0
            )
            for some in (range(lefts), range(lefts, count))
        )
        out_ref[i] = lax.dot_general(
            left, right, (((0,), (0,)), ((), ())), preferred_element_type=jnp.float32
        )


def gram(lefts, rights, near):
    parts = lefts + rights
    layout = tuple((low + (HALF * stride if near else 0), stride) for _, low, stride in parts)
    return pl.pallas_call(
        functools.partial(gram_kernel, layout, len(lefts)),
        in_specs=[pl.BlockSpec(memory_space=pl.ANY)] * len(parts),
        out_specs=pl.BlockSpec(memory_space=pltpu.VMEM),
        out_shape=jax.ShapeDtypeStruct((HALF, BLOCK, BLOCK), jnp.float32),
        scratch_shapes=[
            pltpu.VMEM((HALF * stride,) + array.shape[1:], array.dtype) for array, _, stride in parts
        ]
        + [pltpu.SemaphoreType.DMA((len(parts),))],
        compiler_params=pltpu.CompilerParams(vmem_limit_bytes=16 * MIB),
        cost_estimate=pl.CostEstimate(
            flops=2 * HALF * 256 * BLOCK * BLOCK, bytes_accessed=2 * MIB, transcendentals=0
        ),
        name="gram",
    )(*(in_hbm(array) for array, _, _ in parts))


def finish_kernel(first_ref, live_ref, low_ref, low_far_ref, high_ref, high_far_ref, out_ref):
    for i in range(2 * HALF):
        near_ref, far_ref = (low_ref, low_far_ref) if i < HALF else (high_ref, high_far_ref)
        total = (near_ref[i % HALF] + far_ref[i % HALF]) * (1.0 / TOKENS)
        out_ref[i] = jnp.where(first_ref[0] + i < live_ref[0], total, 0.0)


def finish(first, live, low, low_far, high, high_far):
    return pl.pallas_call(
        finish_kernel,
        in_specs=[pl.BlockSpec(memory_space=pltpu.SMEM)] * 2
        + [pl.BlockSpec(memory_space=pltpu.VMEM)] * 4,
        out_specs=pl.BlockSpec(memory_space=pltpu.VMEM),
        out_shape=jax.ShapeDtypeStruct((2 * HALF, BLOCK, BLOCK), jnp.float32),
        compiler_params=pltpu.CompilerParams(vmem_limit_bytes=16 * MIB),
        cost_estimate=pl.CostEstimate(flops=MIB, bytes_accessed=3 * MIB, transcendentals=0),
        name="finish",
    )(first, live, low, low_far, high, high_far)


def positions(pair_blocks, group_blocks):
    source = pair_blocks // group_blocks
    within = pair_blocks % group_blocks
    slots = pair_blocks.shape[0]
    order = jnp.arange(slots)
    same = source[:, None, :] == source[None, :, :]
    before = (order[None, :] < order[:, None])[:, :, None]
    rank = jnp.sum(same & before, axis=1, dtype=jnp.int32)
    position = source * FROM_GROUP + rank
    hit = position[None, :, :] == order[:, None, None]
    table = jnp.sum(jnp.where(hit, within[None, :, :], 0), axis=1, dtype=jnp.int32)
    return position, table


def shift(value, axis, size, by):
    return lax.ppermute(value, axis, [(i, (i + by) % size) for i in range(size)])


def gather_z(acts):
    spread = jnp.broadcast_to(acts[None], (RANKS,) + acts.shape)
    return lax.all_to_all(spread, "z", 0, 0, tiled=True)


def ring_of_four(value, axis):
    return [value] + [shift(value, axis, SIDE, k) for k in range(1, SIDE)]


def gather_chips(rows):
    width = rows.shape[1] // 2
    left, right = rows[:, :width], rows[:, width:]
    left_x = jnp.stack(ring_of_four(left, "x"))
    right_y = jnp.stack(ring_of_four(right, "y"))
    left_all = jnp.stack(ring_of_four(left_x, "y"))
    right_all = jnp.stack(ring_of_four(right_y, "x"), axis=1)
    return jnp.concatenate([left_all, right_all], axis=3).reshape(-1, rows.shape[1])


def shards(
    acts_early,
    acts_late,
    enc_early,
    enc_late,
    bias_early,
    bias_late,
    thresh_early,
    thresh_late,
    pair_blocks,
    live_pairs,
):
    y, x, c, z = (lax.axis_index(name).astype(jnp.int32) for name in ALL)
    depth = acts_early.shape[1]
    width = enc_early.shape[1]
    rank_blocks = width // BLOCK
    group_blocks = RANKS * rank_blocks

    near = gather_z(jnp.stack([acts_early, acts_late]))
    rows_early = near[:, 0].reshape(-1, depth)
    rows_late = near[:, 1].reshape(-1, depth)
    position, table = positions(pair_blocks, group_blocks)
    lists = jnp.zeros((rows_late.shape[0], BLOCK), jnp.bfloat16).at[:2].set(table.T.astype(jnp.bfloat16))
    all_late = lax.all_gather(
        jnp.concatenate([rows_late, lists], axis=1), LAT, axis=0, tiled=True
    )
    group = (y * SIDE + x) * 2 + c
    asked = all_late.reshape(GROUPS, -1, depth + BLOCK)[:, :2, depth:]
    asked = lax.dynamic_slice_in_dim(asked, group * FROM_GROUP, FROM_GROUP, axis=2)
    asked = jnp.swapaxes(asked, 1, 2).reshape(GROUPS * FROM_GROUP, 2).astype(jnp.int32)
    asked_late = ((z - asked[:, 1] // rank_blocks) & (RANKS - 1)) * rank_blocks + (
        asked[:, 1] % rank_blocks
    )

    own = gather_chips(rows_early)
    step = jnp.arange(CHIPS, dtype=jnp.int32)
    chip = ((y - step // SIDE) & (SIDE - 1)) * SIDE + ((x - step) & (SIDE - 1))
    place = jnp.stack([chip // 2, (chip & 1) * 32 + c * 16], axis=1).reshape(-1)

    def spread(sent):
        got = lax.all_to_all(
            sent.reshape((GROUPS, FROM_GROUP) + sent.shape[1:]),
            LAT,
            split_axis=0,
            concat_axis=0,
            tiled=True,
        )
        return got.reshape(sent.shape)

    offsets = []
    for side in range(2):
        for k in range(REACH + 1):
            by = k if side == 0 else -k
            past = by + (1 if side == 0 else -1)
            offsets += [(past, side), (by, 1 - side)]
    plane = jnp.array([by for by, half in offsets], jnp.int32)
    half = jnp.array([half for by, half in offsets], jnp.int32)
    slots = ((z + plane) & (RANKS - 1)) * (2 * HALF) + half * HALF

    def trade(parts, k):
        return [shift(part, "z", RANKS, by) for part, by in zip(parts, (k, -k))]

    shape = (rank_blocks, TOKENS // RANKS, BLOCK)
    other = shift(own, "c", 2, 1)
    codes_early = encode(
        early_kernel, "encode_early", place, (own, other), enc_early, bias_early, thresh_early,
        jax.ShapeDtypeStruct((RANKS,) + shape, jnp.bfloat16),
    )
    codes_early = lax.all_to_all(codes_early, "z", split_axis=0, concat_axis=0, tiled=True)
    codes_late = encode(
        late_kernel, "encode_late", z[None], (all_late,), enc_late, bias_late, thresh_late,
        [jax.ShapeDtypeStruct(shape, jnp.bfloat16)] * RANKS,
        [pltpu.VMEM((TOKENS, STEP), jnp.bfloat16)],
    )
    codes_early, codes_late = lax.optimization_barrier((codes_early, codes_late))
    sent_early = pick(asked[:, 0], codes_early.reshape((group_blocks,) + shape[1:]), EARLY_PIECES)
    sent_early, codes_late = lax.optimization_barrier((sent_early, codes_late))
    codes_late = [codes_late[0]] + [shift(codes_late[k], "z", RANKS, k) for k in range(1, RANKS)]
    sent_late = pick(asked_late, jnp.concatenate(codes_late), LATE_PIECES)

    def both(parts, k):
        return parts[k], parts[k + REACH + 1]

    sent = list(sent_early) + list(sent_late)
    fine = (-1, TOKENS // RANKS // LATE_PIECES, BLOCK)
    held, extras, traded = [], [], None
    for n in range(len(sent)):
        late = n >= EARLY_PIECES
        got = spread(sent[n])
        if n == EARLY_PIECES - 1:
            got, sent[n + 1 :] = lax.optimization_barrier((got, sent[n + 1 :]))
        if traded is not None:
            traded, got = lax.optimization_barrier((traded, got))
            held[-1].update(traded)
        first_late = n == EARLY_PIECES
        parts = route(slots, position[:, int(late)], got, extras if first_late else ())
        if n + 1 < len(sent):
            sent[n + 1], parts = lax.optimization_barrier((sent[n + 1], parts))
        traded = {k: trade(both(parts, k), k) for k in (3, 2)}
        held.append({0: both(parts, 0), **traded})
        if late:
            held[-1][1] = trade(both(parts, 1), 1)
        else:
            extras += [part.reshape(fine) for part in both(parts, 1)]

    def layer(side, late):
        out = []
        for k in range(REACH + 1):
            at = 0
            rows = 2 * HALF * (LATE_PIECES if k == 1 and not late else EARLY_PIECES) // EARLY_PIECES
            for n in range(EARLY_PIECES if not late else LATE_PIECES):
                if late:
                    low = 2 * HALF * LATE_PIECES if k == 1 and n == 0 else 0
                    out.append((held[EARLY_PIECES + n][k][side], low, 1))
                elif k == 1:
                    out.append((held[EARLY_PIECES][1][side], at, rows // (2 * HALF)))
                    at += rows
                else:
                    out.append((held[n][k][side], 0, 1))
        return out

    def tiles(side, near):
        return gram(layer(side, False), layer(side, True), near)

    low_far = shift(tiles(0, False), "z", RANKS, 1)
    high_far = shift(tiles(1, False), "z", RANKS, -1)
    high = tiles(0, True)
    low = tiles(1, True)
    return finish((z * (2 * HALF))[None], live_pairs, low, low_far, high, high_far)


def solution(mesh):
    fine = Mesh(mesh.devices.reshape(SIDE, SIDE, 2, RANKS), ALL)
    in_specs = (
        P(ALL, None),
        P(ALL, None),
        P(None, ALL),
        P(None, ALL),
        P(ALL),
        P(ALL),
        P(ALL),
        P(ALL),
        P(LAT, None),
        P(LAT),
    )
    out_specs = P(ALL, None, None)
    return jax.shard_map(shards, mesh=fine, in_specs=in_specs, out_specs=out_specs, check_vma=False)
```

```python
import functools

import jax
import jax.numpy as jnp
from jax import lax
from jax.experimental import pallas as pl
from jax.experimental.pallas import tpu as pltpu
from jax.sharding import Mesh, PartitionSpec as P

BLOCK = 128
FROM_GROUP = 4
GROUPS = 32
RANKS = 8
TOKENS = 512
SIDE = 4
CHIPS = SIDE * SIDE
HALF = 8
REACH = 3
STEP = 256
PICKS = 4
EARLY_PIECES = 1
LATE_PIECES = 1
ORDER = (3, 7, 2, 6, 1, 5, 0, 4)
ALL = ("y", "x", "c", "z")
LAT = ("y", "x", "c")
MIB = 1 << 20


def in_hbm(array):
    return pltpu.with_memory_space_constraint(array, pltpu.HBM)


def activate(preact, bias, thresh):
    preact = preact + bias
    return (preact * jnp.clip(2.0 * preact / thresh - 1.0, 0.0, 1.0)).astype(jnp.bfloat16)


def early_kernel(place_ref, own_ref, other_ref, w_ref, bias_ref, thresh_ref, out_ref):
    piece = own_ref.shape[0] // CHIPS
    for side, acts_ref in enumerate((own_ref, other_ref)):
        preact = jnp.dot(acts_ref[...], w_ref[...], preferred_element_type=jnp.float32)
        codes = activate(preact, bias_ref[...], thresh_ref[...])
        for u in range(CHIPS):
            rank = place_ref[2 * u]
            at = pl.multiple_of(place_ref[2 * u + 1] ^ (side * piece), piece)
            for j in range(out_ref.shape[1]):
                out_ref[rank, j, pl.ds(at, piece), :] = codes[
                    u * piece : (u + 1) * piece, j * BLOCK : (j + 1) * BLOCK
                ]


def late_kernel(plane_ref, acts_ref, w_ref, bias_ref, thresh_ref, *refs):
    codes_ref = refs[-1]
    piece = acts_ref.shape[0] // RANKS
    preact = jnp.dot(acts_ref[...], w_ref[...], preferred_element_type=jnp.float32)
    codes_ref[...] = activate(preact, bias_ref[...], thresh_ref[...])
    for k in range(RANKS):
        at = pl.multiple_of(((plane_ref[0] + k) % RANKS) * piece, piece)
        codes = codes_ref[pl.ds(at, piece), :]
        for j in range(refs[k].shape[0]):
            refs[k][j] = codes[:, j * BLOCK : (j + 1) * BLOCK]


def encode(kernel, name, scalar, acts, weight, bias_vec, thresh, out_shape, scratch=()):
    depth, width = weight.shape
    outs = jax.tree.leaves(out_shape)
    specs = [
        pl.BlockSpec((STEP // BLOCK,) + out.shape[1:], lambda i, s: (i, 0, 0))
        if out.ndim == 3
        else pl.BlockSpec(out.shape[:1] + (STEP // BLOCK,) + out.shape[2:], lambda i, s: (0, i, 0, 0))
        for out in outs
    ]
    return pl.pallas_call(
        kernel,
        grid_spec=pltpu.PrefetchScalarGridSpec(
            num_scalar_prefetch=1,
            grid=(width // STEP,),
            in_specs=[pl.BlockSpec((one.shape[0], depth), lambda i, s: (0, 0)) for one in acts]
            + [pl.BlockSpec((depth, STEP), lambda i, s: (0, i))]
            + [pl.BlockSpec((1, STEP), lambda i, s: (0, i))] * 2,
            out_specs=specs if isinstance(out_shape, list) else specs[0],
            scratch_shapes=scratch,
        ),
        out_shape=out_shape,
        compiler_params=pltpu.CompilerParams(vmem_limit_bytes=24 * MIB),
        cost_estimate=pl.CostEstimate(
            flops=2 * TOKENS * depth * width, bytes_accessed=8 * MIB, transcendentals=0
        ),
        name=name,
    )(scalar, *acts, in_hbm(weight), bias_vec[None], thresh[None])


def pick_kernel(index_ref, blocks_ref, *refs):
    outs, (buf_ref, sems) = refs[:-2], refs[-2:]
    chunk = index_ref.shape[0] // PICKS
    tokens = outs[0].shape[1]
    copies = []
    for n, out_ref in enumerate(outs):
        for part in range(PICKS):
            for i in range(part * chunk, (part + 1) * chunk):
                buf_ref[n, i] = blocks_ref[index_ref[i], n * tokens : (n + 1) * tokens, :]
            at = pl.ds(part * chunk, chunk)
            copies.append(
                pltpu.make_async_copy(buf_ref.at[n, at], out_ref.at[at], sems.at[n * PICKS + part])
            )
            copies[-1].start()
    for copy in copies:
        copy.wait()


def pick(index, blocks, pieces):
    count, (tokens, width) = index.shape[0], blocks.shape[1:]
    shape = (count, tokens // pieces, width)
    return pl.pallas_call(
        pick_kernel,
        in_specs=[
            pl.BlockSpec(memory_space=pltpu.SMEM),
            pl.BlockSpec(memory_space=pltpu.VMEM),
        ],
        out_specs=[pl.BlockSpec(memory_space=pltpu.HBM)] * pieces,
        out_shape=[pltpu.HBM(shape, blocks.dtype)] * pieces,
        scratch_shapes=[
            pltpu.VMEM((pieces,) + shape, blocks.dtype),
            pltpu.SemaphoreType.DMA((pieces * PICKS,)),
        ],
        compiler_params=pltpu.CompilerParams(vmem_limit_bytes=16 * MIB),
        cost_estimate=pl.CostEstimate(flops=0, bytes_accessed=3 * MIB, transcendentals=0),
        name="pick",
    )(index, blocks)


def route_kernel(slot_ref, at_ref, blocks_ref, *refs):
    outs, buf_ref, sems = refs[:-2], refs[-2], refs[-1]
    copies = []
    for n in ORDER:
        for part in range(2):
            first = slot_ref[2 * n + part]
            for i in range(HALF):
                buf_ref[n, part * HALF + i] = blocks_ref[at_ref[first + i]]
        copies.append(pltpu.make_async_copy(buf_ref.at[n], outs[n], sems.at[n]))
        copies[-1].start()
    for copy in copies:
        copy.wait()


def route(slot, at, blocks):
    count = 2 * (REACH + 1)
    shape = (2 * HALF,) + blocks.shape[1:]
    return pl.pallas_call(
        route_kernel,
        in_specs=[
            pl.BlockSpec(memory_space=pltpu.SMEM),
            pl.BlockSpec(memory_space=pltpu.SMEM),
            pl.BlockSpec(memory_space=pltpu.VMEM),
        ],
        out_specs=[pl.BlockSpec(memory_space=pltpu.HBM)] * count,
        out_shape=[pltpu.HBM(shape, blocks.dtype)] * count,
        scratch_shapes=[
            pltpu.VMEM((count,) + shape, blocks.dtype),
            pltpu.SemaphoreType.DMA((count,)),
        ],
        compiler_params=pltpu.CompilerParams(vmem_limit_bytes=16 * MIB),
        cost_estimate=pl.CostEstimate(flops=0, bytes_accessed=4 * MIB, transcendentals=0),
        name="route",
    )(slot, at, blocks)


def join_kernel(*refs):
    ins, outs, (buf_ref, sems) = refs[:4], refs[4:6], refs[6:]
    rows = ins[0].shape[0]
    copies = [pltpu.make_async_copy(ins[n], buf_ref.at[n], sems.at[n]) for n in range(4)]
    for copy in copies:
        copy.start()
    for n in range(4):
        copies[n].wait()
        copies.append(
            pltpu.make_async_copy(
                buf_ref.at[n], outs[n // 2].at[pl.ds(n % 2 * rows, rows)], sems.at[4 + n]
            )
        )
        copies[-1].start()
    for copy in copies[4:]:
        copy.wait()


def join(parts):
    shape = parts[0].shape
    out = pltpu.HBM((2 * shape[0],) + shape[1:], parts[0].dtype)
    return pl.pallas_call(
        join_kernel,
        in_specs=[pl.BlockSpec(memory_space=pl.ANY)] * 4,
        out_specs=[pl.BlockSpec(memory_space=pltpu.HBM)] * 2,
        out_shape=[out] * 2,
        scratch_shapes=[
            pltpu.VMEM((4,) + shape, parts[0].dtype),
            pltpu.SemaphoreType.DMA((8,)),
        ],
        compiler_params=pltpu.CompilerParams(vmem_limit_bytes=8 * MIB),
        cost_estimate=pl.CostEstimate(flops=0, bytes_accessed=2 * MIB, transcendentals=0),
        name="join",
    )(*map(in_hbm, parts))


def gram_kernel(layout, lefts, *refs):
    count = len(layout)
    sources, out_ref, bufs, sems = refs[:count], refs[count], refs[count + 1 : -1], refs[-1]
    copies = []
    for n, (low, stride) in enumerate(layout):
        copies.append(
            pltpu.make_async_copy(sources[n].at[pl.ds(low, HALF * stride)], bufs[n], sems.at[n])
        )
        copies[-1].start()
    for copy in copies:
        copy.wait()
    for i in range(HALF):
        left, right = (
            jnp.concatenate(
                [bufs[n][i * layout[n][1] + j] for n in some for j in range(layout[n][1])], axis=0
            )
            for some in (range(lefts), range(lefts, count))
        )
        out_ref[i] = lax.dot_general(
            left, right, (((0,), (0,)), ((), ())), preferred_element_type=jnp.float32
        )


def gram(lefts, rights, near):
    parts = lefts + rights
    layout = tuple((low + (HALF * stride if near else 0), stride) for _, low, stride in parts)
    return pl.pallas_call(
        functools.partial(gram_kernel, layout, len(lefts)),
        in_specs=[pl.BlockSpec(memory_space=pl.ANY)] * len(parts),
        out_specs=pl.BlockSpec(memory_space=pltpu.VMEM),
        out_shape=jax.ShapeDtypeStruct((HALF, BLOCK, BLOCK), jnp.float32),
        scratch_shapes=[
            pltpu.VMEM((HALF * stride,) + array.shape[1:], array.dtype) for array, _, stride in parts
        ]
        + [pltpu.SemaphoreType.DMA((len(parts),))],
        compiler_params=pltpu.CompilerParams(vmem_limit_bytes=16 * MIB),
        cost_estimate=pl.CostEstimate(
            flops=2 * HALF * 256 * BLOCK * BLOCK, bytes_accessed=2 * MIB, transcendentals=0
        ),
        name="gram",
    )(*(in_hbm(array) for array, _, _ in parts))


def finish_kernel(first_ref, live_ref, low_ref, low_far_ref, high_ref, high_far_ref, out_ref):
    for i in range(2 * HALF):
        near_ref, far_ref = (low_ref, low_far_ref) if i < HALF else (high_ref, high_far_ref)
        total = (near_ref[i % HALF] + far_ref[i % HALF]) * (1.0 / TOKENS)
        out_ref[i] = jnp.where(first_ref[0] + i < live_ref[0], total, 0.0)


def finish(first, live, low, low_far, high, high_far):
    return pl.pallas_call(
        finish_kernel,
        in_specs=[pl.BlockSpec(memory_space=pltpu.SMEM)] * 2
        + [pl.BlockSpec(memory_space=pltpu.VMEM)] * 4,
        out_specs=pl.BlockSpec(memory_space=pltpu.VMEM),
        out_shape=jax.ShapeDtypeStruct((2 * HALF, BLOCK, BLOCK), jnp.float32),
        compiler_params=pltpu.CompilerParams(vmem_limit_bytes=16 * MIB),
        cost_estimate=pl.CostEstimate(flops=MIB, bytes_accessed=3 * MIB, transcendentals=0),
        name="finish",
    )(first, live, low, low_far, high, high_far)


def positions(pair_blocks, group_blocks):
    source = pair_blocks // group_blocks
    within = pair_blocks % group_blocks
    slots = pair_blocks.shape[0]
    order = jnp.arange(slots)
    same = source[:, None, :] == source[None, :, :]
    before = (order[None, :] < order[:, None])[:, :, None]
    rank = jnp.sum(same & before, axis=1, dtype=jnp.int32)
    position = source * FROM_GROUP + rank
    hit = position[None, :, :] == order[:, None, None]
    table = jnp.sum(jnp.where(hit, within[None, :, :], 0), axis=1, dtype=jnp.int32)
    return position, table


def shift(value, axis, size, by):
    return lax.ppermute(value, axis, [(i, (i + by) % size) for i in range(size)])


def gather_z(acts):
    spread = jnp.broadcast_to(acts[None], (RANKS,) + acts.shape)
    return lax.all_to_all(spread, "z", 0, 0, tiled=True)


def ring_of_four(value, axis):
    return [value] + [shift(value, axis, SIDE, k) for k in range(1, SIDE)]


def gather_chips(rows):
    width = rows.shape[1] // 2
    left, right = rows[:, :width], rows[:, width:]
    left_x = jnp.stack(ring_of_four(left, "x"))
    right_y = jnp.stack(ring_of_four(right, "y"))
    left_all = jnp.stack(ring_of_four(left_x, "y"))
    right_all = jnp.stack(ring_of_four(right_y, "x"), axis=1)
    return jnp.concatenate([left_all, right_all], axis=3).reshape(-1, rows.shape[1])


def shards(
    acts_early,
    acts_late,
    enc_early,
    enc_late,
    bias_early,
    bias_late,
    thresh_early,
    thresh_late,
    pair_blocks,
    live_pairs,
):
    y, x, c, z = (lax.axis_index(name).astype(jnp.int32) for name in ALL)
    depth = acts_early.shape[1]
    width = enc_early.shape[1]
    rank_blocks = width // BLOCK
    group_blocks = RANKS * rank_blocks

    near = gather_z(jnp.stack([acts_early, acts_late]))
    rows_early = near[:, 0].reshape(-1, depth)
    rows_late = near[:, 1].reshape(-1, depth)
    position, table = positions(pair_blocks, group_blocks)
    lists = jnp.zeros((rows_late.shape[0], BLOCK), jnp.bfloat16).at[:2].set(table.T.astype(jnp.bfloat16))
    all_late = lax.all_gather(
        jnp.concatenate([rows_late, lists], axis=1), LAT, axis=0, tiled=True
    )
    group = (y * SIDE + x) * 2 + c
    asked = all_late.reshape(GROUPS, -1, depth + BLOCK)[:, :2, depth:]
    asked = lax.dynamic_slice_in_dim(asked, group * FROM_GROUP, FROM_GROUP, axis=2)
    asked = jnp.swapaxes(asked, 1, 2).reshape(GROUPS * FROM_GROUP, 2).astype(jnp.int32)
    asked_late = ((z - asked[:, 1] // rank_blocks) & (RANKS - 1)) * rank_blocks + (
        asked[:, 1] % rank_blocks
    )

    own = gather_chips(rows_early)
    step = jnp.arange(CHIPS, dtype=jnp.int32)
    chip = ((y - step // SIDE) & (SIDE - 1)) * SIDE + ((x - step) & (SIDE - 1))
    place = jnp.stack([chip // 2, (chip & 1) * 32 + c * 16], axis=1).reshape(-1)

    def spread(sent):
        got = lax.all_to_all(
            sent.reshape((GROUPS, FROM_GROUP) + sent.shape[1:]),
            LAT,
            split_axis=0,
            concat_axis=0,
            tiled=True,
        )
        return got.reshape(sent.shape)

    offsets = []
    for side in range(2):
        for k in range(REACH + 1):
            by = k if side == 0 else -k
            past = by + (1 if side == 0 else -1)
            offsets += [(past, side), (by, 1 - side)]
    plane = jnp.array([by for by, half in offsets], jnp.int32)
    half = jnp.array([half for by, half in offsets], jnp.int32)
    slots = ((z + plane) & (RANKS - 1)) * (2 * HALF) + half * HALF

    def trade(parts, k):
        return [shift(part, "z", RANKS, by) for part, by in zip(parts, (k, -k))]

    shape = (rank_blocks, TOKENS // RANKS, BLOCK)
    other = shift(own, "c", 2, 1)
    codes_early = encode(
        early_kernel, "encode_early", place, (own, other), enc_early, bias_early, thresh_early,
        jax.ShapeDtypeStruct((RANKS,) + shape, jnp.bfloat16),
    )
    codes_early = lax.all_to_all(codes_early, "z", split_axis=0, concat_axis=0, tiled=True)
    codes_late = encode(
        late_kernel, "encode_late", z[None], (all_late,), enc_late, bias_late, thresh_late,
        [jax.ShapeDtypeStruct(shape, jnp.bfloat16)] * RANKS,
        [pltpu.VMEM((TOKENS, STEP), jnp.bfloat16)],
    )
    codes_early, codes_late = lax.optimization_barrier((codes_early, codes_late))
    sent_early = pick(asked[:, 0], codes_early.reshape((group_blocks,) + shape[1:]), EARLY_PIECES)
    sent_early, codes_late = lax.optimization_barrier((sent_early, codes_late))
    codes_late = [codes_late[0]] + [shift(codes_late[k], "z", RANKS, k) for k in range(1, RANKS)]
    sent_late = pick(asked_late, jnp.concatenate(codes_late), LATE_PIECES)

    def both(parts, k):
        return parts[k], parts[k + REACH + 1]

    sent = list(sent_early) + list(sent_late)
    held, extras, traded = [], None, None
    for n in range(len(sent)):
        late = n >= EARLY_PIECES
        got = spread(sent[n])
        if n == EARLY_PIECES - 1:
            got, sent[n + 1 :] = lax.optimization_barrier((got, sent[n + 1 :]))
        if traded is not None:
            traded, got = lax.optimization_barrier((traded, got))
            held[-1].update(traded)
        parts = route(slots, position[:, int(late)], got)
        if n + 1 < len(sent):
            sent[n + 1], parts = lax.optimization_barrier((sent[n + 1], parts))
        traded = {k: trade(both(parts, k), k) for k in (3, 2)}
        held.append({0: both(parts, 0), **traded})
        if late:
            low, high = both(parts, 1)
            held[-1][1] = trade(join((extras[0], low, extras[1], high)), 1)
        else:
            extras = both(parts, 1)

    def layer(side, late):
        out = []
        for k in range(REACH + 1):
            at = 0
            rows = 2 * HALF * (LATE_PIECES if k == 1 and not late else EARLY_PIECES) // EARLY_PIECES
            for n in range(EARLY_PIECES if not late else LATE_PIECES):
                if late:
                    low = 2 * HALF * LATE_PIECES if k == 1 and n == 0 else 0
                    out.append((held[EARLY_PIECES + n][k][side], low, 1))
                elif k == 1:
                    out.append((held[EARLY_PIECES][1][side], at, rows // (2 * HALF)))
                    at += rows
                else:
                    out.append((held[n][k][side], 0, 1))
        return out

    def tiles(side, near):
        return gram(layer(side, False), layer(side, True), near)

    low_far = shift(tiles(0, False), "z", RANKS, 1)
    high_far = shift(tiles(1, False), "z", RANKS, -1)
    high = tiles(0, True)
    low = tiles(1, True)
    return finish((z * (2 * HALF))[None], live_pairs, low, low_far, high, high_far)


def solution(mesh):
    fine = Mesh(mesh.devices.reshape(SIDE, SIDE, 2, RANKS), ALL)
    in_specs = (
        P(ALL, None),
        P(ALL, None),
        P(None, ALL),
        P(None, ALL),
        P(ALL),
        P(ALL),
        P(ALL),
        P(ALL),
        P(LAT, None),
        P(LAT),
    )
    out_specs = P(ALL, None, None)
    return jax.shard_map(shards, mesh=fine, in_specs=in_specs, out_specs=out_specs, check_vma=False)
```
